32 devices in a mesh: bin: 8 (over y, x, core), trk: 4 (over z).
Axes of the slice: x: 2, y: 2, z: 4, core: 2. Of those that a mesh axis runs over, the one named last changes fastest.
Arguments:
- trunk: bfloat16 [2048, 1536], P(('bin', 'trk')), may hold values from -6 to 6
- norm_gain: float32 [1536], replicated, may hold values from 0.1 to 1.9
- w_query: bfloat16 [1536, 1024], replicated, may hold values from -0.4375 to 0.4375
- w_kv: bfloat16 [1536, 256], replicated, may hold values from -0.15625 to 0.15625
- w_out: bfloat16 [1024, 1536], replicated, may hold values from -0.1875 to 0.1875
- w_up: bfloat16 [1536, 768], replicated, may hold values from -0.15625 to 0.15625
- skip: bfloat16 [8192, 768], P(('bin', 'trk')), may hold values from -6 to 6
- conv_w: bfloat16 [5, 768, 768], replicated, may hold values from -0.09375 to 0.09375
- head_w: bfloat16 [768, 3072], P(None, 'trk'), may hold values from -0.21875 to 0.21875
- head_bias: float32 [3072], P('trk'), may hold values from -4 to 4
- targets: bfloat16 [8192, 3072], P('bin', 'trk'), may hold values from 0.049804688 to 4
- missing: int32 [2048], P('bin'), may hold values 0 or 1
- group_ids: int32 [3072, 1], replicated, may hold values from 0 to 10
- group_weight: float32 [11], replicated, may hold values from 0.25 to 4
Outputs:
- prediction: bfloat16 [8192, 3072], P('bin', 'trk')
- head_grad: float32 [768, 3072], P('bin', 'trk')
- feature_grad: bfloat16 [8192, 768], P(('bin', 'trk'))
The draws below stay inside these ranges and needn't reach their ends.
Inputs may be any that keep to these rules, and one draw needn't show every extreme that they name: `group_ids`: every group id is held by at least one track.
All inputs are finite; a program needn't handle non-finite values. No bound on the sum of `missing` on one device may be relied on, other than what follows from the above.
Results may differ from the reference program's by a relative error of at most 0.019.
Values may be sent and summed in bfloat16 or wider, within the bound.
A program may use at most 128 MiB of HBM per device.

```python
import math
import jax
import jax.numpy as jnp
from jax import lax

C = 1536
HEADS = 8
DK = 128
C2 = 768
KW = 5
UP = 4
GROUPS = 11
TR_DEV = 768
NB = 2048
NP = 8192
TRACKS = 3072
N_TRK = 4


def place_ends(drawn, stream_key, least, high):
    shape = drawn.shape
    place = [jax.random.randint(jax.random.fold_in(stream_key, axis), (), 0, shape[axis]) for axis in range(len(shape))]
    drawn = drawn.at[tuple(place)].set(least)
    longest = shape.index(max(shape))
    place[longest] = (place[longest] + 1) % shape[longest]
    return drawn.at[tuple(place)].set(high)


def steps_of(rng, extent, shards, low, largest):
    level, own = 1.0, jax.random.fold_in(rng, 6)
    for axis_at, shards_of in shards:
        draws = jnp.exp(jax.random.uniform(jax.random.fold_in(own, axis_at), (shards_of,), jnp.float32, low / len(shards), largest / len(shards)))
        level = level * jnp.repeat(draws, extent[axis_at] // shards_of).reshape([-1 if axis == axis_at else 1 for axis in range(len(extent))])
    return level


def distinct(key, rows, amount, top, lift):
    sequence = jax.random.permutation(jax.random.fold_in(key, 1), amount)
    pull = sequence
    for power in range(3):
        pull = pull * pull // amount
    pull = pull * lift // amount
    lots = jax.random.randint(jax.random.fold_in(key, 2), (rows, amount), 0, 4096) + pull
    sure = jax.random.permutation(jax.random.fold_in(key, 3), rows)[jnp.arange(amount) % rows]
    lots = jnp.where(jnp.arange(rows)[:, None] == sure[None, :], 1 << 14, lots)
    score = lots * amount + jnp.arange(amount)
    return lax.top_k(score.astype(jnp.int32), top)[1].astype(jnp.int32)


def bell_draw(stream_key, extent, deviation, reach, pieces=(), kind=jnp.bfloat16):
    entries = jax.random.normal(stream_key, extent, jnp.float32) * deviation
    if len(pieces) > 0:
        entries = steps_of(stream_key, extent, pieces, -0.22, 0.18) * entries
    return jnp.clip(entries, min=-reach, max=reach).astype(kind)


def setup_inputs(seed: int = 0) -> dict:
    splits = jax.random.split(jax.random.key(seed), 15)
    trunk = bell_draw(splits[0], (NB, C), 1.0, 6.0, ((0, 32),))
    norm_gain = jnp.clip(1.0 + 0.18 * jax.random.normal(splits[1], (C,), jnp.float32), 0.1, 1.9)
    w_query = bell_draw(splits[2], (C, HEADS * DK), (C // 9) ** -0.5, 0.4375)
    w_kv = bell_draw(splits[3], (C, 2 * DK), C ** -0.5, 0.15625)
    w_out = bell_draw(splits[4], (HEADS * DK, C), (HEADS * DK) ** -0.5, 0.1875)
    w_up = bell_draw(splits[5], (C, C2), C ** -0.5, 0.15625)
    skip = bell_draw(splits[6], (NP, C2), 1.0, 6.0, ((0, 32),))
    conv_w = bell_draw(splits[7], (KW, C2, C2), (KW * C2) ** -0.5, 0.09375)
    head_w = bell_draw(splits[8], (C2, TRACKS), C2 ** -0.5, 0.21875, ((1, 4),))
    head_bias = bell_draw(splits[9], (TRACKS,), 1.0, 4.0, ((0, 4),), jnp.float32)
    targets = jnp.clip(jnp.exp(math.log(4.0) - 4.3859405 * jax.random.uniform(splits[10], (NP, TRACKS), jnp.float32) ** steps_of(splits[10], (NP, TRACKS), ((0, 8), (1, 4)), -0.2, 0.2)), 0.049804688, 4.0).astype(jnp.bfloat16)
    missing = place_ends((jax.random.randint(splits[11], (NB,), 0, 8) < 1).astype(jnp.int32), jax.random.fold_in(splits[11], 1), 0, 1)
    group_ids = distinct(splits[12], TRACKS, GROUPS, 1, 744)
    group_weight = jnp.clip(jnp.exp(jax.random.uniform(splits[13], (GROUPS,), jnp.float32, math.log(0.25), math.log(4.0))), 0.25, 4.0)
    return {"trunk": trunk, "norm_gain": norm_gain, "w_query": w_query, "w_kv": w_kv, "w_out": w_out, "w_up": w_up, "skip": skip, "conv_w": conv_w, "head_w": head_w, "head_bias": head_bias, "targets": targets, "missing": missing, "group_ids": group_ids, "group_weight": group_weight}


logit_cap = 20.0

def reference(trunk, norm_gain, w_query, w_kv, w_out, w_up, skip, conv_w, head_w, head_bias, targets, missing, group_ids, group_weight):
    widened = trunk.astype(jnp.float32)
    meansq = lax.optimization_barrier(jnp.mean(widened * widened, axis=1, keepdims=True))
    normed = (widened * lax.rsqrt(meansq + 1e-06) * norm_gain).astype(jnp.bfloat16)
    queries = jnp.dot(normed, w_query, preferred_element_type=jnp.float32).astype(jnp.bfloat16)
    keyvals = jnp.dot(normed, w_kv, preferred_element_type=jnp.float32).astype(jnp.bfloat16)
    key_rows = keyvals[:, :DK].astype(jnp.float32)
    value_rows = keyvals[:, DK:].astype(jnp.float32)
    block_rows = math.gcd(NB, 512)
    query_blocks = queries.reshape(NB // block_rows, block_rows, HEADS, DK)
    score_scale = 1.0 / math.sqrt(DK)

    def attend(query_block):
        scores = jnp.einsum('qhd,nd->qhn', query_block.astype(jnp.float32), key_rows) * score_scale
        scores = logit_cap * jnp.tanh(scores / logit_cap)
        exp_weights = jnp.exp(scores)
        denominator = lax.optimization_barrier(jnp.sum(exp_weights, axis=2))
        rounded = lax.optimization_barrier(exp_weights.astype(jnp.bfloat16)).astype(jnp.float32)
        numerator = jnp.einsum('qhn,nd->qhd', rounded, value_rows)
        return (numerator / denominator[:, :, None]).astype(jnp.bfloat16)
    attended = lax.map(attend, query_blocks).reshape(NB, HEADS * DK)
    hidden = (widened + jnp.dot(attended, w_out, preferred_element_type=jnp.float32)).astype(jnp.bfloat16)
    upward = jnp.dot(hidden, w_up, preferred_element_type=jnp.float32)
    upsampled = (jnp.repeat(upward, UP, axis=0) + skip.astype(jnp.float32)).astype(jnp.bfloat16)
    rim_width = KW // 2
    padded = jnp.pad(upsampled, ((rim_width, rim_width), (0, 0)))
    conved = jnp.zeros((NP, C2), jnp.float32)
    for tap in range(KW):
        conved = conved + jnp.dot(padded[tap:tap + NP], conv_w[tap], preferred_element_type=jnp.float32)
    feature = (upsampled.astype(jnp.float32) + jax.nn.gelu(conved)).astype(jnp.bfloat16)
    labels = jnp.arange(GROUPS, dtype=jnp.int32)
    member = group_ids == labels[None, :]
    counts = lax.optimization_barrier(jnp.sum(member.astype(jnp.int32), axis=0))
    per_group = group_weight * TRACKS / (GROUPS * counts.astype(jnp.float32))
    track_scale = lax.optimization_barrier(jnp.sum(jnp.where(member, per_group[None, :], 0.0), axis=1))
    keep_mask = 1.0 - jnp.repeat(missing.astype(jnp.float32), UP)[:, None]
    weight_tiles = head_w.reshape(C2, N_TRK, TR_DEV).transpose(1, 0, 2)
    bias_tiles = head_bias.reshape(N_TRK, TR_DEV)
    target_tiles = targets.reshape(NP, N_TRK, TR_DEV).transpose(1, 0, 2)
    scale_tiles = track_scale.reshape(N_TRK, TR_DEV)

    def head_tile(grad_sum, tile_data):
        tile_weight, tile_bias, tile_target, tile_scale = tile_data
        logits = jnp.dot(feature, tile_weight, preferred_element_type=jnp.float32) + tile_bias
        smooth = jax.nn.softplus(logits)
        misfit = smooth - tile_target.astype(jnp.float32)
        slope_grad = (keep_mask * tile_scale[None, :] * misfit * jax.nn.sigmoid(logits)).astype(jnp.bfloat16)
        weight_grad = jnp.dot(feature.T, slope_grad, preferred_element_type=jnp.float32) / NP
        partial_value = jnp.dot(slope_grad, tile_weight.T, preferred_element_type=jnp.float32)
        partial_value = lax.optimization_barrier(partial_value.astype(jnp.bfloat16)).astype(jnp.float32)
        return (grad_sum + partial_value, (smooth.astype(jnp.bfloat16), weight_grad))
    grad_sum, (pred_tiles, grad_tiles) = lax.scan(head_tile, jnp.zeros((NP, C2), jnp.float32), (weight_tiles, bias_tiles, target_tiles, scale_tiles))
    prediction = pred_tiles.transpose(1, 0, 2).reshape(NP, TRACKS)
    head_grad = grad_tiles.transpose(1, 0, 2).reshape(C2, TRACKS)
    return (prediction, head_grad, grad_sum.astype(jnp.bfloat16))
```

```python
import functools
import math

import jax
import jax.numpy as jnp
from jax import lax
from jax.experimental import pallas as pl
from jax.experimental.pallas import tpu as pltpu
from jax.sharding import PartitionSpec as P

CAP = 20.0
F32 = jnp.float32
BF16 = jnp.bfloat16
NT = (((1,), (1,)), ((), ()))
TN = (((0,), (0,)), ((), ()))


def xor(x, y, size):
    out, bit = 0, 1
    while bit < size:
        a = lax.rem(lax.div(x, bit), 2)
        if isinstance(y, int):
            if (y // bit) % 2:
                a = 1 - a
        else:
            c = lax.rem(lax.div(y, bit), 2)
            a = a + c - 2 * a * c
        out = out + a * bit
        bit *= 2
    return out


def dot(a, b):
    return jnp.dot(a, b, preferred_element_type=F32)


def kernel(
    nb, nt, positions,
    trunk, gain, bias, scale, missing,
    wq, wkv, wout, wup, skip, convw, headw, targets,
    pred, hgrad, fgrad,
    wq_v, wkv_v, wout_v, wup_v, conv_v, head_v, targ_v,
    skip_all, kv_all, q_v, acc_v, den_v, norm_v, hid_v, up_all, u32, win, xs, feat, slope,
    part, part_in, hg, hg_in, hs, hs_in,
    load_sem, pred_sem,
    skip_s, skip_r, kv1_s, kv1_r, kv2_s, kv2_r, kv3_s, kv3_r, up_s, up_r,
    halo_s, halo_r, part_s, part_r, hg_s, hg_r, hs_s, hs_r,
):
    b, t = lax.axis_index("bin"), lax.axis_index("trk")
    rows, chan = trunk.shape
    dk = wkv.shape[1] // 2
    heads = wq.shape[1] // dk
    npos, c2 = skip.shape
    tracks = headw.shape[1]
    taps = convw.shape[0]
    rim = taps // 2
    factor = npos // rows
    group = nt * npos
    half = nb // 2
    tile = 256

    def send(src, dst, ssem, rsem, bb, tt):
        return pltpu.make_async_remote_copy(
            src_ref=src, dst_ref=dst, send_sem=ssem, recv_sem=rsem,
            device_id=(bb, tt), device_id_type=pl.DeviceIdType.MESH,
        )

    loads = [
        pltpu.make_async_copy(src, dst, load_sem.at[i])
        for i, (src, dst) in enumerate([
            (wkv, wkv_v), (wq, wq_v), (wout, wout_v), (wup, wup_v),
            (skip, skip_all.at[t]), (convw, conv_v), (headw, head_v), (targets, targ_v),
        ])
    ]
    for load in loads:
        load.start()

    barrier = pltpu.get_barrier_semaphore()
    greet = [(b, xor(t, o, nt)) for o in range(1, nt)]
    greet += [(xor(b, 2 * j, nb), t) for j in range(1, half)]
    greet += [(lax.rem(b + 1, nb), t), (lax.rem(b + nb - 1, nb), t)]
    for dev in greet:
        pl.semaphore_signal(barrier, inc=1, device_id=dev, device_id_type=pl.DeviceIdType.MESH)
    pl.semaphore_wait(barrier, len(greet))

    core = xor(b, 1, nb)
    skip_c = [
        send(skip, skip_all.at[t], skip_s.at[o], skip_r.at[o], b, xor(t, o, nt)) for o in range(1, nt)
    ]
    for copy in skip_c:
        copy.start()

    wide = trunk[...].astype(F32)
    meansq = jnp.mean(wide * wide, axis=1, keepdims=True)
    norm_v[...] = (wide * lax.rsqrt(meansq + 1e-06) * gain[...]).astype(BF16)
    loads[0].wait()
    kv_all[b, t] = dot(norm_v[...], wkv_v[...]).astype(BF16)
    kv1 = [
        send(kv_all.at[b, t], kv_all.at[b, t], kv1_s.at[o], kv1_r.at[o], b, xor(t, o, nt))
        for o in range(1, nt)
    ]
    for copy in kv1:
        copy.start()

    loads[1].wait()
    per = tile // dk
    for i in range(heads // per):
        res = dot(norm_v[...], wq_v[:, i * tile:(i + 1) * tile]).astype(BF16)
        for k in range(per):
            h = i * per + k
            q_v[h * rows:(h + 1) * rows, :] = res[:, k * dk:(k + 1) * dk]

    for copy in kv1:
        copy.wait_recv()
    kv2 = [
        send(kv_all.at[b], kv_all.at[b], kv2_s.at[j], kv2_r.at[j], xor(b, 2 * j, nb), t)
        for j in range(1, half)
    ]
    for copy in kv2:
        copy.start()
    kv3 = []
    for j in range(half):
        if j:
            kv2[j - 1].wait_recv()
        g = xor(b, 2 * j, nb)
        copy = send(kv_all.at[g], kv_all.at[g], kv3_s.at[j], kv3_r.at[j], core, t)
        copy.start()
        kv3.append(copy)

    acc_v[...] = jnp.zeros_like(acc_v)
    den_v[...] = jnp.zeros_like(den_v)
    score_scale = 1.0 / math.sqrt(dk)

    def fold(g):
        kv = kv_all[g].reshape(nt * rows, 2 * dk)
        s = lax.dot_general(q_v[...], kv[:, :dk], NT, preferred_element_type=F32)
        e = jnp.exp(CAP * jnp.tanh(s * (score_scale / CAP)))
        acc_v[...] += dot(e.astype(BF16), kv[:, dk:])
        d = e[:, :dk]
        for k in range(1, nt * rows // dk):
            d = d + e[:, k * dk:(k + 1) * dk]
        den_v[...] += d

    def fold_own(j, carry):
        fold(xor(b, 2 * j, nb))
        return carry

    def fold_core(j, carry):
        fold(xor(core, 2 * j, nb))
        return carry

    lax.fori_loop(0, half, fold_own, 0)
    for copy in kv3:
        copy.wait_recv()
    lax.fori_loop(0, half, fold_core, 0)

    att = (acc_v[...] / jnp.sum(den_v[...], axis=1, keepdims=True)).astype(BF16)
    for h in range(heads):
        norm_v[:, h * dk:(h + 1) * dk] = att[h * rows:(h + 1) * rows, :]
    loads[2].wait()
    for i in range(chan // tile):
        cols = slice(i * tile, (i + 1) * tile)
        hid_v[:, cols] = (
            trunk[:, cols].astype(F32) + dot(norm_v[:, :heads * dk], wout_v[:, cols])
        ).astype(BF16)
    loads[3].wait()
    for i in range(c2 // tile):
        cols = slice(i * tile, (i + 1) * tile)
        up_all[t, :, cols] = dot(hid_v[...], wup_v[:, cols]).astype(BF16)
    ups = [
        send(up_all.at[t], up_all.at[t], up_s.at[o], up_r.at[o], b, xor(t, o, nt)) for o in range(1, nt)
    ]
    for copy in ups:
        copy.start()

    loads[4].wait()
    for copy in skip_c:
        copy.wait_recv()
    for copy in ups:
        copy.wait_recv()
    spread = (
        lax.broadcasted_iota(jnp.int32, (npos, rows), 0) // factor
        == lax.broadcasted_iota(jnp.int32, (npos, rows), 1)
    ).astype(F32).astype(BF16)

    def assemble(c, carry):
        u = (dot(spread, up_all[c]) + skip_all[c].astype(F32)).astype(BF16).astype(F32)
        u32[pl.ds(pl.multiple_of(8 + c * npos, 8), npos), :] = u
        return carry

    lax.fori_loop(0, nt, assemble, 0)
    to_next = send(
        u32.at[pl.ds(group, 8)], u32.at[pl.ds(0, 8)], halo_s.at[0], halo_r.at[0], lax.rem(b + 1, nb), t
    )
    to_prev = send(
        u32.at[pl.ds(8, 8)], u32.at[pl.ds(8 + group, 8)], halo_s.at[1], halo_r.at[1],
        lax.rem(b + nb - 1, nb), t,
    )
    zeros = jnp.zeros((8, c2), F32)

    @pl.when(b < nb - 1)
    def _():
        to_next.start()

    @pl.when(b > 0)
    def _():
        to_prev.start()

    @pl.when(b == 0)
    def _():
        u32[0:8, :] = zeros

    @pl.when(b == nb - 1)
    def _():
        u32[8 + group:16 + group, :] = zeros

    @pl.when(b > 0)
    def _():
        to_next.wait_recv()

    @pl.when(b < nb - 1)
    def _():
        to_prev.wait_recv()

    for i in range(5, 8):
        loads[i].wait()

    def head_step(i, carry):
        o = nt - 1 - i
        c = xor(t, o, nt)
        base = pl.multiple_of(c * npos, npos)
        win[...] = u32[pl.ds(base, npos + 16), :]
        for k in range(taps):
            xs[k] = win[8 + k - rim:8 + k - rim + npos, :].astype(BF16)
        for n in range(c2 // tile):
            cols = slice(n * tile, (n + 1) * tile)
            acc = dot(xs[0], conv_v[0, :, cols])
            for k in range(1, taps):
                acc = acc + dot(xs[k], conv_v[k, :, cols])
            gelu = 0.5 * acc * (1.0 + jnp.tanh(math.sqrt(2.0 / math.pi) * (acc + 0.044715 * acc * acc * acc)))
            feat[pl.ds(base, npos), cols] = (
                u32[pl.ds(pl.multiple_of(base + 8, 8), npos), cols] + gelu
            ).astype(BF16)
        f = feat[pl.ds(base, npos), :]
        span = missing.shape[1]
        pick = (
            (lax.broadcasted_iota(jnp.int32, (npos, span), 0) + base) // factor
            == lax.broadcasted_iota(jnp.int32, (npos, span), 1)
        ).astype(F32).astype(BF16)
        keep_row = (1 - missing[...]).astype(F32).astype(BF16)
        keep = lax.dot_general(
            pick, jnp.broadcast_to(keep_row, (128, span)), NT, preferred_element_type=F32
        )
        keep = jnp.concatenate([keep] * (tile // 128), axis=1)
        for n in range(tracks // tile):
            cols = slice(n * tile, (n + 1) * tile)
            x = dot(f, head_v[:, cols]) + bias[:, cols]
            e = jnp.exp(-jnp.abs(x))
            u = 1.0 + e
            r = 1.0 / u
            smooth = jnp.maximum(x, 0.0) + (jnp.log(u) + (e - (u - 1.0)) * r)
            sig = jnp.where(x >= 0, r, e * r)
            misfit = smooth - targ_v[pl.ds(base, npos), cols].astype(F32)
            slope[pl.ds(base, npos), cols] = (keep * scale[:, cols] * misfit * sig).astype(BF16)
            targ_v[pl.ds(base, npos), cols] = smooth.astype(BF16)
        pltpu.make_async_copy(
            targ_v.at[pl.ds(base, npos)], pred.at[pl.ds(base, npos)], pred_sem.at[i]
        ).start()
        g = slope[pl.ds(base, npos), :]
        for n in range(c2 // tile):
            cols = slice(n * tile, (n + 1) * tile)
            part[o, :, cols] = lax.dot_general(
                g, head_v[cols, :], NT, preferred_element_type=F32
            ).astype(BF16)

        @pl.when(o > 0)
        def _():
            send(part.at[o], part_in.at[o], part_s.at[o], part_r.at[o], b, c).start()

        return carry

    lax.fori_loop(0, nt, head_step, 0)

    block = c2 // nb
    for n in range(c2 // tile):
        rws = slice(n * tile, (n + 1) * tile)
        for m in range(tracks // tile):
            cols = slice(m * tile, (m + 1) * tile)
            hg[rws, cols] = (
                lax.dot_general(feat[:, rws], slope[:, cols], TN, preferred_element_type=F32)
                * (1.0 / positions)
            ).astype(BF16)
    mine = lax.div(b, 2)
    odd = lax.rem(b, 2)
    hgs = []
    for j in range(half):
        row = pl.multiple_of((2 * j + 1 - odd) * block, block)
        copy = send(hg.at[pl.ds(row, block)], hg_in.at[j], hg_s.at[j], hg_r.at[j], core, t)
        copy.start()
        hgs.append(copy)
    for copy in hgs:
        copy.wait_recv()
    hss = []
    for j in range(1, half):
        q = xor(b, 2 * j, nb)
        row = pl.multiple_of(q * block, block)
        hs[j] = (hg[pl.ds(row, block), :].astype(F32) + hg_in[lax.div(q, 2)].astype(F32)).astype(BF16)
        copy = send(hs.at[j], hs_in.at[j], hs_s.at[j], hs_r.at[j], q, t)
        copy.start()
        hss.append(copy)
    own = hg[pl.ds(pl.multiple_of(b * block, block), block), :].astype(F32) + hg_in[mine].astype(F32)
    for j in range(1, half):
        hss[j - 1].wait_recv()
        own = own + hs_in[j].astype(F32)
    hgrad[...] = own

    total = part[0].astype(F32)
    for o in range(1, nt):
        send(part.at[o], part_in.at[o], part_s.at[o], part_r.at[o], b, xor(t, o, nt)).wait_recv()
        total = total + part_in[o].astype(F32)
    fgrad[...] = total.astype(BF16)

    for o in range(1, nt):
        send(part.at[o], part_in.at[o], part_s.at[o], part_r.at[o], b, xor(t, o, nt)).wait_send()
    for copy in skip_c + kv1 + kv2 + kv3 + ups + hgs + hss:
        copy.wait_send()

    @pl.when(b < nb - 1)
    def _():
        to_next.wait_send()

    @pl.when(b > 0)
    def _():
        to_prev.wait_send()

    for i in range(nt):
        base = pl.multiple_of(xor(t, nt - 1 - i, nt) * npos, npos)
        pltpu.make_async_copy(
            targ_v.at[pl.ds(base, npos)], pred.at[pl.ds(base, npos)], pred_sem.at[i]
        ).wait()


def body(
    trunk, norm_gain, w_query, w_kv, w_out, w_up, skip, conv_w,
    head_w, head_bias, targets, missing, group_ids, group_weight,
):
    nb, nt = lax.axis_size("bin"), lax.axis_size("trk")
    rows, chan = trunk.shape
    npos, c2 = skip.shape
    tracks = head_w.shape[1]
    dk = w_kv.shape[1] // 2
    heads = w_query.shape[1] // dk
    taps = conv_w.shape[0]
    group = nt * npos
    half = nb // 2
    block = c2 // nb

    groups = group_weight.shape[0]
    total_tracks = group_ids.shape[0]
    labels = jnp.arange(groups, dtype=jnp.int32)
    counts = jnp.sum((group_ids == labels[None, :]).astype(jnp.int32), axis=0)
    per_group = group_weight * total_tracks / (groups * counts.astype(F32))
    local_ids = lax.dynamic_slice_in_dim(group_ids, lax.axis_index("trk") * tracks, tracks, 0)
    track_scale = jnp.sum(jnp.where(local_ids == labels[None, :], per_group[None, :], 0.0), axis=1)

    vm = pl.BlockSpec(memory_space=pltpu.VMEM)
    hbm = pl.BlockSpec(memory_space=pl.ANY)
    V = pltpu.VMEM
    dma = pltpu.SemaphoreType.DMA
    flops = 2 * (
        rows * chan * (heads + 2) * dk + rows * heads * nb * nt * rows * 2 * dk
        + rows * heads * dk * chan + rows * chan * c2 + group * taps * c2 * c2 + 3 * group * c2 * tracks
    )
    return pl.pallas_call(
        functools.partial(kernel, nb, nt, float(group * nb)),
        out_shape=(
            jax.ShapeDtypeStruct((group, tracks), BF16),
            jax.ShapeDtypeStruct((block, tracks), F32),
            jax.ShapeDtypeStruct((npos, c2), BF16),
        ),
        in_specs=[vm] * 5 + [hbm] * 8,
        out_specs=(hbm, vm, vm),
        scratch_shapes=[
            V(w_query.shape, BF16), V(w_kv.shape, BF16), V(w_out.shape, BF16), V(w_up.shape, BF16),
            V(conv_w.shape, BF16), V(head_w.shape, BF16), V((group, tracks), BF16),
            V((nt, npos, c2), BF16), V((nb, nt, rows, 2 * dk), BF16), V((heads * rows, dk), BF16),
            V((heads * rows, dk), F32), V((heads * rows, dk), F32), V((rows, chan), BF16),
            V((rows, chan), BF16), V((nt, rows, c2), BF16), V((group + 16, c2), F32), V((npos + 16, c2), F32),
            V((taps, npos, c2), BF16), V((group, c2), BF16), V((group, tracks), BF16),
            V((nt, npos, c2), BF16), V((nt, npos, c2), BF16), V((c2, tracks), BF16),
            V((half, block, tracks), BF16), V((half, block, tracks), BF16), V((half, block, tracks), BF16),
            dma((8,)), dma((nt,)),
            dma((nt,)), dma((nt,)), dma((nt,)), dma((nt,)), dma((half,)), dma((half,)),
            dma((half,)), dma((half,)), dma((nt,)), dma((nt,)),
            dma((2,)), dma((2,)), dma((nt,)), dma((nt,)), dma((half,)), dma((half,)),
            dma((half,)), dma((half,)),
        ],
        compiler_params=pltpu.CompilerParams(
            collective_id=0, has_side_effects=True, vmem_limit_bytes=60 * 1024 * 1024
        ),
        cost_estimate=pl.CostEstimate(
            flops=flops, bytes_accessed=24 * 1024 * 1024, transcendentals=4 * 1024 * 1024
        ),
    )(
        trunk, norm_gain[None, :], head_bias[None, :], track_scale[None, :], missing[None, :],
        w_query, w_kv, w_out, w_up, skip, conv_w, head_w, targets,
    )


def solution(mesh):
    in_specs = (
        P(("bin", "trk"), None), P(), P(), P(), P(), P(), P(("bin", "trk"), None), P(),
        P(None, "trk"), P("trk"), P("bin", "trk"), P("bin"), P(), P(),
    )
    out_specs = (P("bin", "trk"), P("bin", "trk"), P(("bin", "trk"), None))
    return jax.shard_map(body, mesh=mesh, in_specs=in_specs, out_specs=out_specs, check_vma=False)
```

```python
import functools
import math

import jax
import jax.numpy as jnp
from jax import lax
from jax.experimental import pallas as pl
from jax.experimental.pallas import tpu as pltpu
from jax.sharding import PartitionSpec as P

CAP = 20.0
F32 = jnp.float32
BF16 = jnp.bfloat16
NT = (((1,), (1,)), ((), ()))
TN = (((0,), (0,)), ((), ()))


def xor(x, y, size):
    out, bit = 0, 1
    while bit < size:
        a = lax.rem(lax.div(x, bit), 2)
        if isinstance(y, int):
            if (y // bit) % 2:
                a = 1 - a
        else:
            c = lax.rem(lax.div(y, bit), 2)
            a = a + c - 2 * a * c
        out = out + a * bit
        bit *= 2
    return out


def dot(a, b):
    return jnp.dot(a, b, preferred_element_type=F32)


def kernel(
    nb, nt, positions,
    trunk, packed, missing,
    wq, wkv, wout, wup, skip, convw, headw, targets,
    pred, hgrad, fgrad,
    wq_v, wkv_v, wout_v, wup_v, conv_v, head_v, targ_v,
    skip_all, kv_all, q_v, acc_v, den_v, norm_v, hid_v, up_all, u32, win, xs, feat, slope,
    part, part_in, mid, hg, hg_in, hs, hs_in,
    load_sem, pred_sem,
    skip_s, skip_r, fwd_s, mid_s, mid_r, kv1_s, kv1_r, kv2_s, kv2_r, kv3_s, kv3_r, up_s, up_r,
    halo_s, halo_r, part_s, part_r, hg_s, hg_r, hs_s, hs_r,
):
    b, t = lax.axis_index("bin"), lax.axis_index("trk")
    rows, chan = trunk.shape
    dk = wkv.shape[1] // 2
    heads = wq.shape[1] // dk
    npos, c2 = skip.shape
    tracks = headw.shape[1]
    taps = convw.shape[0] // c2
    rim = taps // 2
    factor = npos // rows
    group = nt * npos
    half = nb // 2
    tile = 256
    gain = packed.at[:, :chan]
    bias = packed.at[:, chan:chan + tracks]
    scale = packed.at[:, chan + tracks:]

    def send(src, dst, ssem, rsem, bb, tt):
        return pltpu.make_async_remote_copy(
            src_ref=src, dst_ref=dst, send_sem=ssem, recv_sem=rsem,
            device_id=(bb, tt), device_id_type=pl.DeviceIdType.MESH,
        )

    loads = [
        pltpu.make_async_copy(src, dst, load_sem.at[i])
        for i, (src, dst) in enumerate([
            (wkv, wkv_v), (wq, wq_v), (wout, wout_v), (wup, wup_v),
            (skip, skip_all.at[t]), (convw, conv_v), (headw, head_v), (targets, targ_v),
        ])
    ]
    for load in loads:
        load.start()

    barrier = pltpu.get_barrier_semaphore()
    greet = [(b, xor(t, o, nt)) for o in range(1, nt)]
    greet += [(xor(b, 2 * j, nb), t) for j in range(1, half)]
    greet += [(lax.rem(b + 1, nb), t), (lax.rem(b + nb - 1, nb), t)]
    for dev in greet:
        pl.semaphore_signal(barrier, inc=1, device_id=dev, device_id_type=pl.DeviceIdType.MESH)
    pl.semaphore_wait(barrier, len(greet))

    core = xor(b, 1, nb)
    pair, todd, mate = lax.div(t, 2), lax.rem(t, 2), xor(t, 1, nt)

    def far_side(j):
        q = xor(pair, j, nt // 2)
        up = jnp.where(q > pair, 1, 0)
        return q, up, todd == up

    skip_c = [send(skip, skip_all.at[t], skip_s.at[0], skip_r.at[1], b, mate)]
    for j in range(1, nt // 2):
        q, up, _ = far_side(j)
        there = 2 * q + 1 - up
        differ = todd + (1 - up) - 2 * todd * (1 - up)
        skip_c.append(send(skip, skip_all.at[t], skip_s.at[j], skip_r.at[2 * j + differ], b, there))
    for copy in skip_c:
        copy.start()

    def passed(o):
        c = xor(t, o, nt)
        return send(skip_all.at[c], skip_all.at[c], fwd_s.at[o], skip_r.at[xor(o, 1, nt)], b, mate)

    def arrival(o):
        return send(skip, skip_all.at[xor(t, o, nt)], skip_s.at[0], skip_r.at[o], b, mate)

    def pass_on(o):
        @pl.when(far_side(o // 2)[2])
        def _():
            arrival(o).wait_recv()
            passed(o).start()

    wide = trunk[...].astype(F32)
    meansq = jnp.mean(wide * wide, axis=1, keepdims=True)
    norm_v[...] = (wide * lax.rsqrt(meansq + 1e-06) * gain[...]).astype(BF16)
    loads[0].wait()
    kv_all[b, t] = dot(norm_v[...], wkv_v[...]).astype(BF16)
    kv1 = [
        send(kv_all.at[b, t], kv_all.at[b, t], kv1_s.at[o], kv1_r.at[o], b, xor(t, o, nt))
        for o in range(1, nt)
    ]
    for copy in kv1:
        copy.start()

    loads[1].wait()
    per = tile // dk
    for i in range(heads // per):
        res = dot(norm_v[...], wq_v[:, i * tile:(i + 1) * tile]).astype(BF16)
        for k in range(per):
            h = i * per + k
            q_v[h * rows:(h + 1) * rows, :] = res[:, k * dk:(k + 1) * dk]

    for copy in kv1:
        copy.wait_recv()
    kv2 = [
        send(kv_all.at[b], kv_all.at[b], kv2_s.at[j], kv2_r.at[j], xor(b, 2 * j, nb), t)
        for j in range(1, half)
    ]
    for copy in kv2:
        copy.start()
    kv3 = []
    for j in range(half):
        if j:
            kv2[j - 1].wait_recv()
        g = xor(b, 2 * j, nb)
        copy = send(kv_all.at[g], kv_all.at[g], kv3_s.at[j], kv3_r.at[j], core, t)
        copy.start()
        kv3.append(copy)

    for o in range(2, nt, 2):
        pass_on(o)
    acc_v[...] = jnp.zeros_like(acc_v)
    den_v[...] = jnp.zeros_like(den_v)
    score_scale = 1.0 / math.sqrt(dk)

    def fold(g):
        kv = kv_all[g].reshape(nt * rows, 2 * dk)
        s = lax.dot_general(q_v[...], kv[:, :dk], NT, preferred_element_type=F32)
        e = jnp.exp(CAP * jnp.tanh(s * (score_scale / CAP)))
        acc_v[...] += dot(e.astype(BF16), kv[:, dk:])
        d = e[:, :dk]
        for k in range(1, nt * rows // dk):
            d = d + e[:, k * dk:(k + 1) * dk]
        den_v[...] += d

    def fold_own(j, carry):
        fold(xor(b, 2 * j, nb))
        return carry

    def fold_core(j, carry):
        fold(xor(core, 2 * j, nb))
        return carry

    lax.fori_loop(0, half, fold_own, 0)
    for copy in kv3:
        copy.wait_recv()
    lax.fori_loop(0, half, fold_core, 0)
    for o in range(3, nt, 2):
        pass_on(o)

    att = (acc_v[...] / jnp.sum(den_v[...], axis=1, keepdims=True)).astype(BF16)
    for h in range(heads):
        norm_v[:, h * dk:(h + 1) * dk] = att[h * rows:(h + 1) * rows, :]
    loads[2].wait()
    for i in range(chan // tile):
        cols = slice(i * tile, (i + 1) * tile)
        hid_v[:, cols] = (
            trunk[:, cols].astype(F32) + dot(norm_v[:, :heads * dk], wout_v[:, cols])
        ).astype(BF16)
    loads[3].wait()
    for i in range(c2 // tile):
        cols = slice(i * tile, (i + 1) * tile)
        up_all[t, :, cols] = dot(hid_v[...], wup_v[:, cols]).astype(BF16)
    ups = [
        send(up_all.at[t], up_all.at[t], up_s.at[o], up_r.at[o], b, xor(t, o, nt)) for o in range(1, nt)
    ]
    for copy in ups:
        copy.start()

    loads[4].wait()
    arrival(1).wait_recv()
    for o in range(2, nt):
        @pl.when(jnp.logical_not(far_side(o // 2)[2]))
        def _():
            arrival(o).wait_recv()
    for copy in ups:
        copy.wait_recv()
    spread = (
        lax.broadcasted_iota(jnp.int32, (npos, rows), 0) // factor
        == lax.broadcasted_iota(jnp.int32, (npos, rows), 1)
    ).astype(F32).astype(BF16)

    def assemble(c, carry):
        u = (dot(spread, up_all[c]) + skip_all[c].astype(F32)).astype(BF16).astype(F32)
        u32[pl.ds(pl.multiple_of(8 + c * npos, 8), npos), :] = u
        return carry

    lax.fori_loop(0, nt, assemble, 0)
    to_next = send(
        u32.at[pl.ds(group, 8)], u32.at[pl.ds(0, 8)], halo_s.at[0], halo_r.at[0], lax.rem(b + 1, nb), t
    )
    to_prev = send(
        u32.at[pl.ds(8, 8)], u32.at[pl.ds(8 + group, 8)], halo_s.at[1], halo_r.at[1],
        lax.rem(b + nb - 1, nb), t,
    )
    zeros = jnp.zeros((8, c2), F32)

    @pl.when(b < nb - 1)
    def _():
        to_next.start()

    @pl.when(b > 0)
    def _():
        to_prev.start()

    @pl.when(b == 0)
    def _():
        u32[0:8, :] = zeros

    @pl.when(b == nb - 1)
    def _():
        u32[8 + group:16 + group, :] = zeros

    @pl.when(b > 0)
    def _():
        to_next.wait_recv()

    @pl.when(b < nb - 1)
    def _():
        to_prev.wait_recv()

    for i in range(5, 8):
        loads[i].wait()

    def is_near(o):
        q = xor(pair, lax.div(o, 2), nt // 2)
        return todd == jnp.where(q > pair, 1, 0)

    def to_mate(o):
        return send(part.at[o], mid.at[o], mid_s.at[o], mid_r.at[o], b, mate)

    def to_owner(o):
        j = lax.div(o, 2)
        return send(part.at[o], part_in.at[j], part_s.at[o], part_r.at[j], b, xor(t, o, nt))

    def head_step(i, carry):
        o = nt - 1 - i
        c = xor(t, o, nt)
        base = pl.multiple_of(c * npos, npos)
        win[...] = u32[pl.ds(base, npos + 16), :]
        for k in range(taps):
            xs[:, k * c2:(k + 1) * c2] = win[8 + k - rim:8 + k - rim + npos, :].astype(BF16)
        for n in range(c2 // tile):
            cols = slice(n * tile, (n + 1) * tile)
            acc = dot(xs[...], conv_v[:, cols])
            gelu = 0.5 * acc * (1.0 + jnp.tanh(math.sqrt(2.0 / math.pi) * (acc + 0.044715 * acc * acc * acc)))
            feat[pl.ds(base, npos), cols] = (
                u32[pl.ds(pl.multiple_of(base + 8, 8), npos), cols] + gelu
            ).astype(BF16)
        f = feat[pl.ds(base, npos), :]
        span = missing.shape[1]
        pick = (
            (lax.broadcasted_iota(jnp.int32, (npos, span), 0) + base) // factor
            == lax.broadcasted_iota(jnp.int32, (npos, span), 1)
        ).astype(F32).astype(BF16)
        keep_row = (1 - missing[...]).astype(F32).astype(BF16)
        keep = lax.dot_general(
            pick, jnp.broadcast_to(keep_row, (128, span)), NT, preferred_element_type=F32
        )
        keep = jnp.concatenate([keep] * (tile // 128), axis=1)
        for n in range(tracks // tile):
            cols = slice(n * tile, (n + 1) * tile)
            x = dot(f, head_v[:, cols]) + bias[:, cols]
            e = jnp.exp(-jnp.abs(x))
            u = 1.0 + e
            r = 1.0 / u
            smooth = jnp.maximum(x, 0.0) + (jnp.log(u) + (e - (u - 1.0)) * r)
            sig = jnp.where(x >= 0, r, e * r)
            misfit = smooth - targ_v[pl.ds(base, npos), cols].astype(F32)
            slope[pl.ds(base, npos), cols] = (keep * scale[:, cols] * misfit * sig).astype(BF16)
            targ_v[pl.ds(base, npos), cols] = smooth.astype(BF16)
        pltpu.make_async_copy(
            targ_v.at[pl.ds(base, npos)], pred.at[pl.ds(base, npos)], pred_sem.at[i]
        ).start()
        g = slope[pl.ds(base, npos), :]
        for n in range(c2 // tile):
            cols = slice(n * tile, (n + 1) * tile)
            part[o, :, cols] = lax.dot_general(
                g, head_v[cols, :], NT, preferred_element_type=F32
            ).astype(BF16)

        @pl.when(o == 1)
        def _():
            to_owner(o).start()

        @pl.when(o >= 2)
        def _():
            @pl.when(jnp.logical_not(is_near(o)))
            def _():
                to_mate(o).start()

        @pl.when(i >= 2)
        def _():
            late = nt + 1 - i

            @pl.when(is_near(late))
            def _():
                to_mate(late).wait_recv()
                z = xor(late, 1, nt)
                part[z] = (part[z].astype(F32) + mid[late].astype(F32)).astype(BF16)
                to_owner(z).start()

        return carry

    lax.fori_loop(0, nt, head_step, 0)

    block = c2 // nb
    for n in range(c2 // tile):
        rws = slice(n * tile, (n + 1) * tile)
        for m in range(tracks // tile):
            cols = slice(m * tile, (m + 1) * tile)
            hg[rws, cols] = (
                lax.dot_general(feat[:, rws], slope[:, cols], TN, preferred_element_type=F32)
                * (1.0 / positions)
            ).astype(BF16)
    mine = lax.div(b, 2)
    odd = lax.rem(b, 2)
    hgs = []
    for j in range(half):
        row = pl.multiple_of((2 * j + 1 - odd) * block, block)
        copy = send(hg.at[pl.ds(row, block)], hg_in.at[j], hg_s.at[j], hg_r.at[j], core, t)
        copy.start()
        hgs.append(copy)
    for copy in hgs:
        copy.wait_recv()
    hss = []
    for j in range(1, half):
        q = xor(b, 2 * j, nb)
        row = pl.multiple_of(q * block, block)
        hs[j] = (hg[pl.ds(row, block), :].astype(F32) + hg_in[lax.div(q, 2)].astype(F32)).astype(BF16)
        copy = send(hs.at[j], hs_in.at[j], hs_s.at[j], hs_r.at[j], q, t)
        copy.start()
        hss.append(copy)
    own = hg[pl.ds(pl.multiple_of(b * block, block), block), :].astype(F32) + hg_in[mine].astype(F32)
    for j in range(1, half):
        hss[j - 1].wait_recv()
        own = own + hs_in[j].astype(F32)
    hgrad[...] = own

    total = part[0].astype(F32)
    for j in range(nt // 2):
        to_owner(max(2 * j, 1)).wait_recv()
        total = total + part_in[j].astype(F32)
    fgrad[...] = total.astype(BF16)

    to_owner(1).wait_send()
    for o in range(2, nt):
        @pl.when(far_side(o // 2)[2])
        def _():
            to_owner(o).wait_send()
            passed(o).wait_send()

        @pl.when(jnp.logical_not(far_side(o // 2)[2]))
        def _():
            to_mate(o).wait_send()
    for copy in skip_c + kv1 + kv2 + kv3 + ups + hgs + hss:
        copy.wait_send()

    @pl.when(b < nb - 1)
    def _():
        to_next.wait_send()

    @pl.when(b > 0)
    def _():
        to_prev.wait_send()

    for i in range(nt):
        base = pl.multiple_of(xor(t, nt - 1 - i, nt) * npos, npos)
        pltpu.make_async_copy(
            targ_v.at[pl.ds(base, npos)], pred.at[pl.ds(base, npos)], pred_sem.at[i]
        ).wait()


def body(
    trunk, norm_gain, w_query, w_kv, w_out, w_up, skip, conv_w,
    head_w, head_bias, targets, missing, group_ids, group_weight,
):
    nb, nt = lax.axis_size("bin"), lax.axis_size("trk")
    rows, chan = trunk.shape
    npos, c2 = skip.shape
    tracks = head_w.shape[1]
    dk = w_kv.shape[1] // 2
    heads = w_query.shape[1] // dk
    taps = conv_w.shape[0]
    group = nt * npos
    half = nb // 2
    block = c2 // nb

    groups = group_weight.shape[0]
    total_tracks = group_ids.shape[0]
    labels = jnp.arange(groups, dtype=jnp.int32)
    counts = jnp.sum((group_ids == labels[None, :]).astype(jnp.int32), axis=0)
    per_group = group_weight * total_tracks / (groups * counts.astype(F32))
    local_ids = lax.dynamic_slice_in_dim(group_ids, lax.axis_index("trk") * tracks, tracks, 0)
    track_scale = jnp.sum(jnp.where(local_ids == labels[None, :], per_group[None, :], 0.0), axis=1)

    vm = pl.BlockSpec(memory_space=pltpu.VMEM)
    hbm = pl.BlockSpec(memory_space=pl.ANY)
    V = pltpu.VMEM
    dma = pltpu.SemaphoreType.DMA
    flops = 2 * (
        rows * chan * (heads + 2) * dk + rows * heads * nb * nt * rows * 2 * dk
        + rows * heads * dk * chan + rows * chan * c2 + group * taps * c2 * c2 + 3 * group * c2 * tracks
    )
    return pl.pallas_call(
        functools.partial(kernel, nb, nt, float(group * nb)),
        out_shape=(
            jax.ShapeDtypeStruct((group, tracks), BF16),
            jax.ShapeDtypeStruct((block, tracks), F32),
            jax.ShapeDtypeStruct((npos, c2), BF16),
        ),
        in_specs=[vm] * 3 + [hbm] * 8,
        out_specs=(hbm, vm, vm),
        scratch_shapes=[
            V(w_query.shape, BF16), V(w_kv.shape, BF16), V(w_out.shape, BF16), V(w_up.shape, BF16),
            V((taps * c2, c2), BF16), V(head_w.shape, BF16), V((group, tracks), BF16),
            V((nt, npos, c2), BF16), V((nb, nt, rows, 2 * dk), BF16), V((heads * rows, dk), BF16),
            V((heads * rows, dk), F32), V((heads * rows, dk), F32), V((rows, chan), BF16),
            V((rows, chan), BF16), V((nt, rows, c2), BF16), V((group + 16, c2), F32), V((npos + 16, c2), F32),
            V((npos, taps * c2), BF16), V((group, c2), BF16), V((group, tracks), BF16),
            V((nt, npos, c2), BF16), V((nt // 2, npos, c2), BF16), V((nt, npos, c2), BF16), V((c2, tracks), BF16),
            V((half, block, tracks), BF16), V((half, block, tracks), BF16), V((half, block, tracks), BF16),
            dma((8,)), dma((nt,)), dma((nt,)), dma((nt,)), dma((nt,)),
            dma((nt,)), dma((nt,)), dma((nt,)), dma((nt,)), dma((half,)), dma((half,)),
            dma((half,)), dma((half,)), dma((nt,)), dma((nt,)),
            dma((2,)), dma((2,)), dma((nt,)), dma((nt,)), dma((half,)), dma((half,)),
            dma((half,)), dma((half,)),
        ],
        compiler_params=pltpu.CompilerParams(
            collective_id=0, has_side_effects=True, vmem_limit_bytes=60 * 1024 * 1024
        ),
        cost_estimate=pl.CostEstimate(
            flops=flops, bytes_accessed=24 * 1024 * 1024, transcendentals=4 * 1024 * 1024
        ),
    )(
        trunk, jnp.concatenate([norm_gain, head_bias, track_scale])[None, :], missing[None, :],
        w_query, w_kv, w_out, w_up, skip, conv_w.reshape(taps * c2, c2), head_w, targets,
    )


def solution(mesh):
    in_specs = (
        P(("bin", "trk"), None), P(), P(), P(), P(), P(), P(("bin", "trk"), None), P(),
        P(None, "trk"), P("trk"), P("bin", "trk"), P("bin"), P(), P(),
    )
    out_specs = (P("bin", "trk"), P("bin", "trk"), P(("bin", "trk"), None))
    return jax.shard_map(body, mesh=mesh, in_specs=in_specs, out_specs=out_specs, check_vma=False)
```

```python
import functools
import math

import jax
import jax.numpy as jnp
from jax import lax
from jax.experimental import pallas as pl
from jax.experimental.pallas import tpu as pltpu
from jax.sharding import PartitionSpec as P

CAP = 20.0
F32 = jnp.float32
BF16 = jnp.bfloat16
NT = (((1,), (1,)), ((), ()))
TN = (((0,), (0,)), ((), ()))


def xor(x, y, size):
    out, bit = 0, 1
    while bit < size:
        a = lax.rem(lax.div(x, bit), 2)
        if isinstance(y, int):
            if (y // bit) % 2:
                a = 1 - a
        else:
            c = lax.rem(lax.div(y, bit), 2)
            a = a + c - 2 * a * c
        out = out + a * bit
        bit *= 2
    return out


def dot(a, b):
    return jnp.dot(a, b, preferred_element_type=F32)


def kernel(
    nb, nt, positions,
    trunk, gain, bias, missing, ids, weight,
    wq, wkv, wout, wup, skip, convw, headw, targets,
    pred, hgrad, fgrad,
    wq_v, wkv_v, wout_v, wup_v, conv_v, head_v, targ_v,
    skip_all, kv_all, q_v, acc_v, den_v, norm_v, hid_v, up_all, u32, win, xs, feat, slope,
    bias_v, scale_v, part, part_in, mid, hg, hg_in, hs, hs_in,
    load_sem, pred_sem,
    skip_s, skip_r, fwd_s, mid_s, mid_r, kv1_s, kv1_r, kv2_s, kv2_r, kv3_s, kv3_r, up_s, up_r,
    halo_s, halo_r, part_s, part_r, hg_s, hg_r, hs_s, hs_r,
):
    b, t = lax.axis_index("bin"), lax.axis_index("trk")
    rows, chan = trunk.shape
    dk = wkv.shape[1] // 2
    heads = wq.shape[1] // dk
    npos, c2 = skip.shape
    tracks = headw.shape[1]
    taps = convw.shape[0] // c2
    rim = taps // 2
    factor = npos // rows
    group = nt * npos
    half = nb // 2
    tile = 256

    def send(src, dst, ssem, rsem, bb, tt):
        return pltpu.make_async_remote_copy(
            src_ref=src, dst_ref=dst, send_sem=ssem, recv_sem=rsem,
            device_id=(bb, tt), device_id_type=pl.DeviceIdType.MESH,
        )

    loads = [
        pltpu.make_async_copy(src, dst, load_sem.at[i])
        for i, (src, dst) in enumerate([
            (wkv, wkv_v), (wq, wq_v), (wout, wout_v), (wup, wup_v),
            (skip, skip_all.at[t]), (convw, conv_v), (headw, head_v), (targets, targ_v),
        ])
    ]
    for load in loads:
        load.start()

    barrier = pltpu.get_barrier_semaphore()
    greet = [(b, xor(t, o, nt)) for o in range(1, nt)]
    greet += [(xor(b, 2 * j, nb), t) for j in range(1, half)]
    greet += [(lax.rem(b + 1, nb), t), (lax.rem(b + nb - 1, nb), t)]
    for dev in greet:
        pl.semaphore_signal(barrier, inc=1, device_id=dev, device_id_type=pl.DeviceIdType.MESH)
    pl.semaphore_wait(barrier, len(greet))

    core = xor(b, 1, nb)
    pair, todd, mate = lax.div(t, 2), lax.rem(t, 2), xor(t, 1, nt)

    def far_side(j):
        q = xor(pair, j, nt // 2)
        up = jnp.where(q > pair, 1, 0)
        return q, up, todd == up

    skip_c = [send(skip, skip_all.at[t], skip_s.at[0], skip_r.at[1], b, mate)]
    for j in range(1, nt // 2):
        q, up, _ = far_side(j)
        there = 2 * q + 1 - up
        differ = todd + (1 - up) - 2 * todd * (1 - up)
        skip_c.append(send(skip, skip_all.at[t], skip_s.at[j], skip_r.at[2 * j + differ], b, there))
    for copy in skip_c:
        copy.start()

    def passed(o):
        c = xor(t, o, nt)
        return send(skip_all.at[c], skip_all.at[c], fwd_s.at[o], skip_r.at[xor(o, 1, nt)], b, mate)

    def arrival(o):
        return send(skip, skip_all.at[xor(t, o, nt)], skip_s.at[0], skip_r.at[o], b, mate)

    def pass_on(o):
        @pl.when(far_side(o // 2)[2])
        def _():
            arrival(o).wait_recv()
            passed(o).start()

    wide = trunk[...].astype(F32)
    meansq = jnp.mean(wide * wide, axis=1, keepdims=True)
    norm_v[...] = (wide * lax.rsqrt(meansq + 1e-06) * gain[...].reshape(1, chan)).astype(BF16)
    loads[0].wait()
    kv_all[b, t] = dot(norm_v[...], wkv_v[...]).astype(BF16)
    kv1 = [
        send(kv_all.at[b, t], kv_all.at[b, t], kv1_s.at[o], kv1_r.at[o], b, xor(t, o, nt))
        for o in range(1, nt)
    ]
    for copy in kv1:
        copy.start()

    loads[1].wait()
    per = tile // dk
    for i in range(heads // per):
        res = dot(norm_v[...], wq_v[:, i * tile:(i + 1) * tile]).astype(BF16)
        for k in range(per):
            h = i * per + k
            q_v[h * rows:(h + 1) * rows, :] = res[:, k * dk:(k + 1) * dk]

    bias_v[...] = bias[...].reshape(1, tracks)
    total_tracks = ids.shape[1]
    groups = weight.shape[0]
    local = ids[:, pl.ds(pl.multiple_of(t * tracks, tracks), tracks)]
    track_scale = jnp.zeros((1, tracks), F32)
    for g in range(groups):
        count = jnp.sum((ids[...] == g).astype(F32), axis=1, keepdims=True)
        track_scale = jnp.where(local == g, weight[g] * total_tracks / (groups * count), track_scale)
    scale_v[...] = track_scale

    for copy in kv1:
        copy.wait_recv()
    kv2 = [
        send(kv_all.at[b], kv_all.at[b], kv2_s.at[j], kv2_r.at[j], xor(b, 2 * j, nb), t)
        for j in range(1, half)
    ]
    for copy in kv2:
        copy.start()
    kv3 = []
    for j in range(half):
        if j:
            kv2[j - 1].wait_recv()
        g = xor(b, 2 * j, nb)
        copy = send(kv_all.at[g], kv_all.at[g], kv3_s.at[j], kv3_r.at[j], core, t)
        copy.start()
        kv3.append(copy)

    for o in range(2, nt, 2):
        pass_on(o)
    acc_v[...] = jnp.zeros_like(acc_v)
    den_v[...] = jnp.zeros_like(den_v)
    score_scale = 1.0 / math.sqrt(dk)

    def fold(g):
        kv = kv_all[g].reshape(nt * rows, 2 * dk)
        s = lax.dot_general(q_v[...], kv[:, :dk], NT, preferred_element_type=F32)
        e = jnp.exp(CAP * jnp.tanh(s * (score_scale / CAP)))
        acc_v[...] += dot(e.astype(BF16), kv[:, dk:])
        d = e[:, :dk]
        for k in range(1, nt * rows // dk):
            d = d + e[:, k * dk:(k + 1) * dk]
        den_v[...] += d

    def fold_own(j, carry):
        fold(xor(b, 2 * j, nb))
        return carry

    def fold_core(j, carry):
        fold(xor(core, 2 * j, nb))
        return carry

    lax.fori_loop(0, half, fold_own, 0)
    for copy in kv3:
        copy.wait_recv()
    lax.fori_loop(0, half, fold_core, 0)
    for o in range(3, nt, 2):
        pass_on(o)

    att = (acc_v[...] / jnp.sum(den_v[...], axis=1, keepdims=True)).astype(BF16)
    for h in range(heads):
        norm_v[:, h * dk:(h + 1) * dk] = att[h * rows:(h + 1) * rows, :]
    loads[2].wait()
    for i in range(chan // tile):
        cols = slice(i * tile, (i + 1) * tile)
        hid_v[:, cols] = (
            trunk[:, cols].astype(F32) + dot(norm_v[:, :heads * dk], wout_v[:, cols])
        ).astype(BF16)
    loads[3].wait()
    for i in range(c2 // tile):
        cols = slice(i * tile, (i + 1) * tile)
        up_all[t, :, cols] = dot(hid_v[...], wup_v[:, cols]).astype(BF16)
    ups = [
        send(up_all.at[t], up_all.at[t], up_s.at[o], up_r.at[o], b, xor(t, o, nt)) for o in range(1, nt)
    ]
    for copy in ups:
        copy.start()

    loads[4].wait()
    arrival(1).wait_recv()
    for o in range(2, nt):
        @pl.when(jnp.logical_not(far_side(o // 2)[2]))
        def _():
            arrival(o).wait_recv()
    for copy in ups:
        copy.wait_recv()
    spread = (
        lax.broadcasted_iota(jnp.int32, (npos, rows), 0) // factor
        == lax.broadcasted_iota(jnp.int32, (npos, rows), 1)
    ).astype(F32).astype(BF16)

    def assemble(c, carry):
        u = (dot(spread, up_all[c]) + skip_all[c].astype(F32)).astype(BF16).astype(F32)
        u32[pl.ds(pl.multiple_of(8 + c * npos, 8), npos), :] = u
        return carry

    lax.fori_loop(0, nt, assemble, 0)
    to_next = send(
        u32.at[pl.ds(group, 8)], u32.at[pl.ds(0, 8)], halo_s.at[0], halo_r.at[0], lax.rem(b + 1, nb), t
    )
    to_prev = send(
        u32.at[pl.ds(8, 8)], u32.at[pl.ds(8 + group, 8)], halo_s.at[1], halo_r.at[1],
        lax.rem(b + nb - 1, nb), t,
    )
    zeros = jnp.zeros((8, c2), F32)

    @pl.when(b < nb - 1)
    def _():
        to_next.start()

    @pl.when(b > 0)
    def _():
        to_prev.start()

    @pl.when(b == 0)
    def _():
        u32[0:8, :] = zeros

    @pl.when(b == nb - 1)
    def _():
        u32[8 + group:16 + group, :] = zeros

    @pl.when(b > 0)
    def _():
        to_next.wait_recv()

    @pl.when(b < nb - 1)
    def _():
        to_prev.wait_recv()

    for i in range(5, 8):
        loads[i].wait()

    def is_near(o):
        q = xor(pair, lax.div(o, 2), nt // 2)
        return todd == jnp.where(q > pair, 1, 0)

    def to_mate(o):
        return send(part.at[o], mid.at[o], mid_s.at[o], mid_r.at[o], b, mate)

    def to_owner(o):
        j = lax.div(o, 2)
        return send(part.at[o], part_in.at[j], part_s.at[o], part_r.at[j], b, xor(t, o, nt))

    def head_step(i, carry):
        o = nt - 1 - i
        c = xor(t, o, nt)
        base = pl.multiple_of(c * npos, npos)
        win[...] = u32[pl.ds(base, npos + 16), :]
        for k in range(taps):
            xs[:, k * c2:(k + 1) * c2] = win[8 + k - rim:8 + k - rim + npos, :].astype(BF16)
        for n in range(c2 // tile):
            cols = slice(n * tile, (n + 1) * tile)
            acc = dot(xs[...], conv_v[:, cols])
            gelu = 0.5 * acc * (1.0 + jnp.tanh(math.sqrt(2.0 / math.pi) * (acc + 0.044715 * acc * acc * acc)))
            feat[pl.ds(base, npos), cols] = (
                u32[pl.ds(pl.multiple_of(base + 8, 8), npos), cols] + gelu
            ).astype(BF16)
        f = feat[pl.ds(base, npos), :]
        span = missing.shape[1]
        pick = (
            (lax.broadcasted_iota(jnp.int32, (npos, span), 0) + base) // factor
            == lax.broadcasted_iota(jnp.int32, (npos, span), 1)
        ).astype(F32).astype(BF16)
        keep_row = (1 - missing[...]).astype(F32).astype(BF16)
        keep = lax.dot_general(
            pick, jnp.broadcast_to(keep_row, (128, span)), NT, preferred_element_type=F32
        )
        keep = jnp.concatenate([keep] * (tile // 128), axis=1)
        for n in range(tracks // tile):
            cols = slice(n * tile, (n + 1) * tile)
            x = dot(f, head_v[:, cols]) + bias_v[:, cols]
            e = jnp.exp(-jnp.abs(x))
            u = 1.0 + e
            r = 1.0 / u
            smooth = jnp.maximum(x, 0.0) + (jnp.log(u) + (e - (u - 1.0)) * r)
            sig = jnp.where(x >= 0, r, e * r)
            misfit = smooth - targ_v[pl.ds(base, npos), cols].astype(F32)
            slope[pl.ds(base, npos), cols] = (keep * scale_v[:, cols] * misfit * sig).astype(BF16)
            targ_v[pl.ds(base, npos), cols] = smooth.astype(BF16)
        pltpu.make_async_copy(
            targ_v.at[pl.ds(base, npos)], pred.at[pl.ds(base, npos)], pred_sem.at[i]
        ).start()
        g = slope[pl.ds(base, npos), :]
        for n in range(c2 // tile):
            cols = slice(n * tile, (n + 1) * tile)
            part[o, :, cols] = lax.dot_general(
                g, head_v[cols, :], NT, preferred_element_type=F32
            ).astype(BF16)

        @pl.when(o == 1)
        def _():
            to_owner(o).start()

        @pl.when(o >= 2)
        def _():
            @pl.when(jnp.logical_not(is_near(o)))
            def _():
                to_mate(o).start()

        @pl.when(i >= 2)
        def _():
            late = nt + 1 - i

            @pl.when(is_near(late))
            def _():
                to_mate(late).wait_recv()
                z = xor(late, 1, nt)
                part[z] = (part[z].astype(F32) + mid[late].astype(F32)).astype(BF16)
                to_owner(z).start()

        return carry

    lax.fori_loop(0, nt, head_step, 0)

    block = c2 // nb
    mine = lax.div(b, 2)
    odd = lax.rem(b, 2)

    def to_core(j):
        row = pl.multiple_of((2 * j + 1 - odd) * block, block)
        return send(hg.at[pl.ds(row, block)], hg_in.at[j], hg_s.at[j], hg_r.at[j], core, t)

    def to_chip(j):
        return send(
            hs.at[j], hs_in.at[xor(mine, j, half)], hs_s.at[j], hs_r.at[xor(mine, j, half)], 2 * j + odd, t
        )

    def chip_sum(j):
        to_core(j).wait_recv()
        row = pl.multiple_of((2 * j + odd) * block, block)
        hs[j] = (hg[pl.ds(row, block), :].astype(F32) + hg_in[j].astype(F32)).astype(BF16)

        @pl.when(mine != j)
        def _():
            to_chip(j).start()

    sent = summed = 0
    for n in range(c2 // tile):
        rws = slice(n * tile, (n + 1) * tile)
        hg[rws, :] = (
            lax.dot_general(feat[:, rws], slope[...], TN, preferred_element_type=F32) * (1.0 / positions)
        ).astype(BF16)
        while summed < sent:
            chip_sum(summed)
            summed += 1
        while sent < half and (2 * sent + 2) * block <= (n + 1) * tile:
            to_core(sent).start()
            sent += 1
    while summed < half:
        chip_sum(summed)
        summed += 1
    own = hs[mine].astype(F32)
    for j in range(1, half):
        send(hs.at[0], hs_in.at[j], hs_s.at[0], hs_r.at[j], core, t).wait_recv()
        own = own + hs_in[j].astype(F32)
    hgrad[...] = own

    total = part[0].astype(F32)
    for j in range(nt // 2):
        to_owner(max(2 * j, 1)).wait_recv()
        total = total + part_in[j].astype(F32)
    fgrad[...] = total.astype(BF16)

    to_owner(1).wait_send()
    for o in range(2, nt):
        @pl.when(far_side(o // 2)[2])
        def _():
            to_owner(o).wait_send()
            passed(o).wait_send()

        @pl.when(jnp.logical_not(far_side(o // 2)[2]))
        def _():
            to_mate(o).wait_send()
    for copy in skip_c + kv1 + kv2 + kv3 + ups:
        copy.wait_send()
    for j in range(half):
        to_core(j).wait_send()

        @pl.when(mine != j)
        def _():
            to_chip(j).wait_send()

    @pl.when(b < nb - 1)
    def _():
        to_next.wait_send()

    @pl.when(b > 0)
    def _():
        to_prev.wait_send()

    for i in range(nt):
        base = pl.multiple_of(xor(t, nt - 1 - i, nt) * npos, npos)
        pltpu.make_async_copy(
            targ_v.at[pl.ds(base, npos)], pred.at[pl.ds(base, npos)], pred_sem.at[i]
        ).wait()


def body(
    trunk, norm_gain, w_query, w_kv, w_out, w_up, skip, conv_w,
    head_w, head_bias, targets, missing, group_ids, group_weight,
):
    nb, nt = lax.axis_size("bin"), lax.axis_size("trk")
    rows, chan = trunk.shape
    npos, c2 = skip.shape
    tracks = head_w.shape[1]
    dk = w_kv.shape[1] // 2
    heads = w_query.shape[1] // dk
    taps = conv_w.shape[0]
    group = nt * npos
    half = nb // 2
    block = c2 // nb

    vm = pl.BlockSpec(memory_space=pltpu.VMEM)
    hbm = pl.BlockSpec(memory_space=pl.ANY)
    V = pltpu.VMEM
    dma = pltpu.SemaphoreType.DMA
    flops = 2 * (
        rows * chan * (heads + 2) * dk + rows * heads * nb * nt * rows * 2 * dk
        + rows * heads * dk * chan + rows * chan * c2 + group * taps * c2 * c2 + 3 * group * c2 * tracks
    )
    return pl.pallas_call(
        functools.partial(kernel, nb, nt, float(group * nb)),
        out_shape=(
            jax.ShapeDtypeStruct((group, tracks), BF16),
            jax.ShapeDtypeStruct((block, tracks), F32),
            jax.ShapeDtypeStruct((npos, c2), BF16),
        ),
        in_specs=[vm] * 5 + [pl.BlockSpec(memory_space=pltpu.SMEM)] + [hbm] * 8,
        out_specs=(hbm, vm, vm),
        scratch_shapes=[
            V(w_query.shape, BF16), V(w_kv.shape, BF16), V(w_out.shape, BF16), V(w_up.shape, BF16),
            V((taps * c2, c2), BF16), V(head_w.shape, BF16), V((group, tracks), BF16),
            V((nt, npos, c2), BF16), V((nb, nt, rows, 2 * dk), BF16), V((heads * rows, dk), BF16),
            V((heads * rows, dk), F32), V((heads * rows, dk), F32), V((rows, chan), BF16),
            V((rows, chan), BF16), V((nt, rows, c2), BF16), V((group + 16, c2), F32), V((npos + 16, c2), F32),
            V((npos, taps * c2), BF16), V((group, c2), BF16), V((group, tracks), BF16),
            V((1, tracks), F32), V((1, tracks), F32),
            V((nt, npos, c2), BF16), V((nt // 2, npos, c2), BF16), V((nt, npos, c2), BF16), V((c2, tracks), BF16),
            V((half, block, tracks), BF16), V((half, block, tracks), BF16), V((half, block, tracks), BF16),
            dma((8,)), dma((nt,)), dma((nt,)), dma((nt,)), dma((nt,)),
            dma((nt,)), dma((nt,)), dma((nt,)), dma((nt,)), dma((half,)), dma((half,)),
            dma((half,)), dma((half,)), dma((nt,)), dma((nt,)),
            dma((2,)), dma((2,)), dma((nt,)), dma((nt,)), dma((half,)), dma((half,)),
            dma((half,)), dma((half,)),
        ],
        compiler_params=pltpu.CompilerParams(
            collective_id=0, has_side_effects=True, vmem_limit_bytes=60 * 1024 * 1024
        ),
        cost_estimate=pl.CostEstimate(
            flops=flops, bytes_accessed=24 * 1024 * 1024, transcendentals=4 * 1024 * 1024
        ),
    )(
        trunk, norm_gain, head_bias, missing[None, :], group_ids.reshape(1, -1), group_weight,
        w_query, w_kv, w_out, w_up, skip, conv_w.reshape(taps * c2, c2), head_w, targets,
    )


def solution(mesh):
    in_specs = (
        P(("bin", "trk"), None), P(), P(), P(), P(), P(), P(("bin", "trk"), None), P(),
        P(None, "trk"), P("trk"), P("bin", "trk"), P("bin"), P(), P(),
    )
    out_specs = (P("bin", "trk"), P("bin", "trk"), P(("bin", "trk"), None))
    return jax.shard_map(body, mesh=mesh, in_specs=in_specs, out_specs=out_specs, check_vma=False)
```

```python
import functools
import math

import jax
import jax.numpy as jnp
from jax import lax
from jax.experimental import pallas as pl
from jax.experimental.pallas import tpu as pltpu
from jax.sharding import PartitionSpec as P

CAP = 20.0
F32 = jnp.float32
BF16 = jnp.bfloat16
NT = (((1,), (1,)), ((), ()))
TN = (((0,), (0,)), ((), ()))


def xor(x, y, size):
    out, bit = 0, 1
    while bit < size:
        a = lax.rem(lax.div(x, bit), 2)
        if isinstance(y, int):
            if (y // bit) % 2:
                a = 1 - a
        else:
            c = lax.rem(lax.div(y, bit), 2)
            a = a + c - 2 * a * c
        out = out + a * bit
        bit *= 2
    return out


def dot(a, b):
    return jnp.dot(a, b, preferred_element_type=F32)


def kernel(
    nb, nt, positions,
    trunk, gain, bias, missing, ids, weight,
    wq, wkv, wout, wup, skip, convw, headw, targets,
    pred, hgrad, fgrad,
    wq_v, wkv_v, wout_v, wup_v, conv_v, head_v, targ_v,
    skip_all, kv_all, q_v, acc_v, den_v, norm_v, hid_v, up_all, u32, win, xs, feat, slope,
    bias_v, scale_v, part, part_in, mid, hg, hg_in, hs, hs_in,
    load_sem, pred_sem,
    skip_s, skip_r, fwd_s, mid_s, mid_r, kv1_s, kv1_r, kv2_s, kv2_r, kv3_s, kv3_r, up_s, up_r,
    halo_s, halo_r, part_s, part_r, hg_s, hg_r, hs_s, hs_r,
):
    b, t = lax.axis_index("bin"), lax.axis_index("trk")
    rows, chan = trunk.shape
    dk = wkv.shape[1] // 2
    heads = wq.shape[1] // dk
    npos, c2 = skip.shape
    tracks = headw.shape[1]
    taps = convw.shape[0] // c2
    rim = taps // 2
    factor = npos // rows
    group = nt * npos
    half = nb // 2
    tile = 256

    def send(src, dst, ssem, rsem, bb, tt):
        return pltpu.make_async_remote_copy(
            src_ref=src, dst_ref=dst, send_sem=ssem, recv_sem=rsem,
            device_id=(bb, tt), device_id_type=pl.DeviceIdType.MESH,
        )

    loads = [
        pltpu.make_async_copy(src, dst, load_sem.at[i])
        for i, (src, dst) in enumerate([
            (wkv, wkv_v), (wq, wq_v), (wout, wout_v), (wup, wup_v),
            (skip, skip_all.at[t]), (convw, conv_v), (headw, head_v), (targets, targ_v),
        ])
    ]
    for load in loads:
        load.start()

    barrier = pltpu.get_barrier_semaphore()
    greet = [(b, xor(t, o, nt)) for o in range(1, nt)]
    greet += [(xor(b, 2 * j, nb), t) for j in range(1, half)]
    greet += [(lax.rem(b + 1, nb), t), (lax.rem(b + nb - 1, nb), t)]
    for dev in greet:
        pl.semaphore_signal(barrier, inc=1, device_id=dev, device_id_type=pl.DeviceIdType.MESH)
    pl.semaphore_wait(barrier, len(greet))

    core = xor(b, 1, nb)
    pair, todd, mate = lax.div(t, 2), lax.rem(t, 2), xor(t, 1, nt)

    def far_side(j):
        q = xor(pair, j, nt // 2)
        up = jnp.where(q > pair, 1, 0)
        return q, up, todd == up

    skip_c = [send(skip, skip_all.at[t], skip_s.at[0], skip_r.at[1], b, mate)]
    for j in range(1, nt // 2):
        q, up, _ = far_side(j)
        there = 2 * q + 1 - up
        differ = todd + (1 - up) - 2 * todd * (1 - up)
        skip_c.append(send(skip, skip_all.at[t], skip_s.at[j], skip_r.at[2 * j + differ], b, there))
    for copy in skip_c:
        copy.start()

    def passed(o):
        c = xor(t, o, nt)
        return send(skip_all.at[c], skip_all.at[c], fwd_s.at[o], skip_r.at[xor(o, 1, nt)], b, mate)

    def arrival(o):
        return send(skip, skip_all.at[xor(t, o, nt)], skip_s.at[0], skip_r.at[o], b, mate)

    def pass_on(o):
        @pl.when(far_side(o // 2)[2])
        def _():
            arrival(o).wait_recv()
            passed(o).start()

    wide = trunk[...].astype(F32)
    meansq = jnp.mean(wide * wide, axis=1, keepdims=True)
    norm_v[...] = (wide * lax.rsqrt(meansq + 1e-06) * gain[...].reshape(1, chan)).astype(BF16)
    loads[0].wait()
    kv_all[b, t] = dot(norm_v[...], wkv_v[...]).astype(BF16)
    kv1 = [
        send(kv_all.at[b, t], kv_all.at[b, t], kv1_s.at[o], kv1_r.at[o], b, xor(t, o, nt))
        for o in range(1, nt)
    ]
    for copy in kv1:
        copy.start()

    loads[1].wait()
    per = tile // dk
    for i in range(heads // per):
        res = dot(norm_v[...], wq_v[:, i * tile:(i + 1) * tile]).astype(BF16)
        for k in range(per):
            h = i * per + k
            q_v[h * rows:(h + 1) * rows, :] = res[:, k * dk:(k + 1) * dk]

    bias_v[...] = bias[...].reshape(1, tracks)
    total_tracks = ids.shape[1]
    groups = weight.shape[0]
    local = ids[:, pl.ds(pl.multiple_of(t * tracks, tracks), tracks)]
    track_scale = jnp.zeros((1, tracks), F32)
    for g in range(groups):
        count = jnp.sum((ids[...] == g).astype(F32), axis=1, keepdims=True)
        track_scale = jnp.where(local == g, weight[g] * total_tracks / (groups * count), track_scale)
    scale_v[...] = track_scale

    for copy in kv1:
        copy.wait_recv()
    kv2 = [
        send(kv_all.at[b], kv_all.at[b], kv2_s.at[j], kv2_r.at[j], xor(b, 2 * j, nb), t)
        for j in range(1, half)
    ]
    for copy in kv2:
        copy.start()
    kv3 = []
    for j in range(half):
        if j:
            kv2[j - 1].wait_recv()
        g = xor(b, 2 * j, nb)
        copy = send(kv_all.at[g], kv_all.at[g], kv3_s.at[j], kv3_r.at[j], core, t)
        copy.start()
        kv3.append(copy)

    for o in range(2, nt, 2):
        pass_on(o)
    acc_v[...] = jnp.zeros_like(acc_v)
    den_v[...] = jnp.zeros_like(den_v)
    score_scale = 1.0 / math.sqrt(dk)

    def fold(g):
        kv = kv_all[g].reshape(nt * rows, 2 * dk)
        s = lax.dot_general(q_v[...], kv[:, :dk], NT, preferred_element_type=F32)
        e = jnp.exp(CAP * jnp.tanh(s * (score_scale / CAP)))
        acc_v[...] += dot(e.astype(BF16), kv[:, dk:])
        d = e[:, :dk]
        for k in range(1, nt * rows // dk):
            d = d + e[:, k * dk:(k + 1) * dk]
        den_v[...] += d

    def fold_own(j, carry):
        fold(xor(b, 2 * j, nb))
        return carry

    def fold_core(j, carry):
        fold(xor(core, 2 * j, nb))
        return carry

    lax.fori_loop(0, half, fold_own, 0)
    for o in range(3, nt, 2):
        pass_on(o)
    for copy in kv3:
        copy.wait_recv()
    lax.fori_loop(0, half, fold_core, 0)

    att = (acc_v[...] / jnp.sum(den_v[...], axis=1, keepdims=True)).astype(BF16)
    for h in range(heads):
        norm_v[:, h * dk:(h + 1) * dk] = att[h * rows:(h + 1) * rows, :]
    loads[2].wait()
    for i in range(chan // tile):
        cols = slice(i * tile, (i + 1) * tile)
        hid_v[:, cols] = (
            trunk[:, cols].astype(F32) + dot(norm_v[:, :heads * dk], wout_v[:, cols])
        ).astype(BF16)
    loads[3].wait()
    for i in range(c2 // tile):
        cols = slice(i * tile, (i + 1) * tile)
        up_all[t, :, cols] = dot(hid_v[...], wup_v[:, cols]).astype(BF16)
    ups = [
        send(up_all.at[t], up_all.at[t], up_s.at[o], up_r.at[o], b, xor(t, o, nt)) for o in range(1, nt)
    ]
    for copy in ups:
        copy.start()

    loads[4].wait()
    arrival(1).wait_recv()
    for o in range(2, nt):
        @pl.when(jnp.logical_not(far_side(o // 2)[2]))
        def _():
            arrival(o).wait_recv()
    for copy in ups:
        copy.wait_recv()
    spread = (
        lax.broadcasted_iota(jnp.int32, (npos, rows), 0) // factor
        == lax.broadcasted_iota(jnp.int32, (npos, rows), 1)
    ).astype(F32).astype(BF16)

    def assemble(c, carry):
        u = (dot(spread, up_all[c]) + skip_all[c].astype(F32)).astype(BF16).astype(F32)
        u32[pl.ds(pl.multiple_of(8 + c * npos, 8), npos), :] = u
        return carry

    lax.fori_loop(0, nt, assemble, 0)
    to_next = send(
        u32.at[pl.ds(group, 8)], u32.at[pl.ds(0, 8)], halo_s.at[0], halo_r.at[0], lax.rem(b + 1, nb), t
    )
    to_prev = send(
        u32.at[pl.ds(8, 8)], u32.at[pl.ds(8 + group, 8)], halo_s.at[1], halo_r.at[1],
        lax.rem(b + nb - 1, nb), t,
    )
    zeros = jnp.zeros((8, c2), F32)

    @pl.when(b < nb - 1)
    def _():
        to_next.start()

    @pl.when(b > 0)
    def _():
        to_prev.start()

    @pl.when(b == 0)
    def _():
        u32[0:8, :] = zeros

    @pl.when(b == nb - 1)
    def _():
        u32[8 + group:16 + group, :] = zeros

    @pl.when(b > 0)
    def _():
        to_next.wait_recv()

    @pl.when(b < nb - 1)
    def _():
        to_prev.wait_recv()

    for i in range(5, 8):
        loads[i].wait()

    def is_near(o):
        q = xor(pair, lax.div(o, 2), nt // 2)
        return todd == jnp.where(q > pair, 1, 0)

    def to_mate(o):
        return send(part.at[o], mid.at[o], mid_s.at[o], mid_r.at[o], b, mate)

    def to_owner(o):
        j = lax.div(o, 2)
        return send(part.at[o], part_in.at[j], part_s.at[o], part_r.at[j], b, xor(t, o, nt))

    def head_step(i, carry):
        o = nt - 1 - i
        c = xor(t, o, nt)
        base = pl.multiple_of(c * npos, npos)
        win[...] = u32[pl.ds(base, npos + 16), :]
        for k in range(taps):
            xs[:, k * c2:(k + 1) * c2] = win[8 + k - rim:8 + k - rim + npos, :].astype(BF16)
        for n in range(c2 // tile):
            cols = slice(n * tile, (n + 1) * tile)
            acc = dot(xs[...], conv_v[:, cols])
            gelu = 0.5 * acc * (1.0 + jnp.tanh(math.sqrt(2.0 / math.pi) * (acc + 0.044715 * acc * acc * acc)))
            feat[pl.ds(base, npos), cols] = (
                u32[pl.ds(pl.multiple_of(base + 8, 8), npos), cols] + gelu
            ).astype(BF16)
        f = feat[pl.ds(base, npos), :]
        span = missing.shape[1]
        pick = (
            (lax.broadcasted_iota(jnp.int32, (npos, span), 0) + base) // factor
            == lax.broadcasted_iota(jnp.int32, (npos, span), 1)
        ).astype(F32).astype(BF16)
        keep_row = (1 - missing[...]).astype(F32).astype(BF16)
        keep = lax.dot_general(
            pick, jnp.broadcast_to(keep_row, (128, span)), NT, preferred_element_type=F32
        )
        keep = jnp.concatenate([keep] * (tile // 128), axis=1)
        for n in range(tracks // tile):
            cols = slice(n * tile, (n + 1) * tile)
            x = dot(f, head_v[:, cols]) + bias_v[:, cols]
            e = jnp.exp(-jnp.abs(x))
            u = 1.0 + e
            r = 1.0 / u
            smooth = jnp.maximum(x, 0.0) + (jnp.log(u) + (e - (u - 1.0)) * r)
            sig = jnp.where(x >= 0, r, e * r)
            misfit = smooth - targ_v[pl.ds(base, npos), cols].astype(F32)
            slope[pl.ds(base, npos), cols] = (keep * scale_v[:, cols] * misfit * sig).astype(BF16)
            targ_v[pl.ds(base, npos), cols] = smooth.astype(BF16)
        pltpu.make_async_copy(
            targ_v.at[pl.ds(base, npos)], pred.at[pl.ds(base, npos)], pred_sem.at[i]
        ).start()
        g = slope[pl.ds(base, npos), :]
        for n in range(c2 // tile):
            cols = slice(n * tile, (n + 1) * tile)
            part[o, :, cols] = lax.dot_general(
                g, head_v[cols, :], NT, preferred_element_type=F32
            ).astype(BF16)

        @pl.when(o == 1)
        def _():
            to_owner(o).start()

        @pl.when(o >= 2)
        def _():
            @pl.when(jnp.logical_not(is_near(o)))
            def _():
                to_mate(o).start()

        @pl.when(i >= 2)
        def _():
            late = nt + 1 - i

            @pl.when(is_near(late))
            def _():
                to_mate(late).wait_recv()
                z = xor(late, 1, nt)
                part[z] = (part[z].astype(F32) + mid[late].astype(F32)).astype(BF16)
                to_owner(z).start()

        return carry

    lax.fori_loop(0, nt, head_step, 0)

    block = c2 // nb
    mine = lax.div(b, 2)
    odd = lax.rem(b, 2)

    def to_core(j):
        row = pl.multiple_of((2 * j + 1 - odd) * block, block)
        return send(hg.at[pl.ds(row, block)], hg_in.at[j], hg_s.at[j], hg_r.at[j], core, t)

    def to_chip(j):
        return send(
            hs.at[j], hs_in.at[xor(mine, j, half)], hs_s.at[j], hs_r.at[xor(mine, j, half)], 2 * j + odd, t
        )

    def chip_sum(j):
        to_core(j).wait_recv()
        row = pl.multiple_of((2 * j + odd) * block, block)
        hs[j] = (hg[pl.ds(row, block), :].astype(F32) + hg_in[j].astype(F32)).astype(BF16)

        @pl.when(mine != j)
        def _():
            to_chip(j).start()

    sent = summed = 0
    for n in range(c2 // tile):
        rws = slice(n * tile, (n + 1) * tile)
        hg[rws, :] = (
            lax.dot_general(feat[:, rws], slope[...], TN, preferred_element_type=F32) * (1.0 / positions)
        ).astype(BF16)
        while summed < sent:
            chip_sum(summed)
            summed += 1
        while sent < half and (2 * sent + 2) * block <= (n + 1) * tile:
            to_core(sent).start()
            sent += 1
    while summed < half:
        chip_sum(summed)
        summed += 1
    own = hs[mine].astype(F32)
    for j in range(1, half):
        send(hs.at[0], hs_in.at[j], hs_s.at[0], hs_r.at[j], core, t).wait_recv()
        own = own + hs_in[j].astype(F32)
    hgrad[...] = own

    total = part[0].astype(F32)
    for j in range(nt // 2):
        to_owner(max(2 * j, 1)).wait_recv()
        total = total + part_in[j].astype(F32)
    fgrad[...] = total.astype(BF16)

    to_owner(1).wait_send()
    for o in range(2, nt):
        @pl.when(far_side(o // 2)[2])
        def _():
            to_owner(o).wait_send()
            passed(o).wait_send()

        @pl.when(jnp.logical_not(far_side(o // 2)[2]))
        def _():
            to_mate(o).wait_send()
    for copy in skip_c + kv1 + kv2 + kv3 + ups:
        copy.wait_send()
    for j in range(half):
        to_core(j).wait_send()

        @pl.when(mine != j)
        def _():
            to_chip(j).wait_send()

    @pl.when(b < nb - 1)
    def _():
        to_next.wait_send()

    @pl.when(b > 0)
    def _():
        to_prev.wait_send()

    for i in range(nt):
        base = pl.multiple_of(xor(t, nt - 1 - i, nt) * npos, npos)
        pltpu.make_async_copy(
            targ_v.at[pl.ds(base, npos)], pred.at[pl.ds(base, npos)], pred_sem.at[i]
        ).wait()


def body(
    trunk, norm_gain, w_query, w_kv, w_out, w_up, skip, conv_w,
    head_w, head_bias, targets, missing, group_ids, group_weight,
):
    nb, nt = lax.axis_size("bin"), lax.axis_size("trk")
    rows, chan = trunk.shape
    npos, c2 = skip.shape
    tracks = head_w.shape[1]
    dk = w_kv.shape[1] // 2
    heads = w_query.shape[1] // dk
    taps = conv_w.shape[0]
    group = nt * npos
    half = nb // 2
    block = c2 // nb

    vm = pl.BlockSpec(memory_space=pltpu.VMEM)
    hbm = pl.BlockSpec(memory_space=pl.ANY)
    V = pltpu.VMEM
    dma = pltpu.SemaphoreType.DMA
    flops = 2 * (
        rows * chan * (heads + 2) * dk + rows * heads * nb * nt * rows * 2 * dk
        + rows * heads * dk * chan + rows * chan * c2 + group * taps * c2 * c2 + 3 * group * c2 * tracks
    )
    return pl.pallas_call(
        functools.partial(kernel, nb, nt, float(group * nb)),
        out_shape=(
            jax.ShapeDtypeStruct((group, tracks), BF16),
            jax.ShapeDtypeStruct((block, tracks), F32),
            jax.ShapeDtypeStruct((npos, c2), BF16),
        ),
        in_specs=[vm] * 5 + [pl.BlockSpec(memory_space=pltpu.SMEM)] + [hbm] * 8,
        out_specs=(hbm, vm, vm),
        scratch_shapes=[
            V(w_query.shape, BF16), V(w_kv.shape, BF16), V(w_out.shape, BF16), V(w_up.shape, BF16),
            V((taps * c2, c2), BF16), V(head_w.shape, BF16), V((group, tracks), BF16),
            V((nt, npos, c2), BF16), V((nb, nt, rows, 2 * dk), BF16), V((heads * rows, dk), BF16),
            V((heads * rows, dk), F32), V((heads * rows, dk), F32), V((rows, chan), BF16),
            V((rows, chan), BF16), V((nt, rows, c2), BF16), V((group + 16, c2), F32), V((npos + 16, c2), F32),
            V((npos, taps * c2), BF16), V((group, c2), BF16), V((group, tracks), BF16),
            V((1, tracks), F32), V((1, tracks), F32),
            V((nt, npos, c2), BF16), V((nt // 2, npos, c2), BF16), V((nt, npos, c2), BF16), V((c2, tracks), BF16),
            V((half, block, tracks), BF16), V((half, block, tracks), BF16), V((half, block, tracks), BF16),
            dma((8,)), dma((nt,)), dma((nt,)), dma((nt,)), dma((nt,)),
            dma((nt,)), dma((nt,)), dma((nt,)), dma((nt,)), dma((half,)), dma((half,)),
            dma((half,)), dma((half,)), dma((nt,)), dma((nt,)),
            dma((2,)), dma((2,)), dma((nt,)), dma((nt,)), dma((half,)), dma((half,)),
            dma((half,)), dma((half,)),
        ],
        compiler_params=pltpu.CompilerParams(
            collective_id=0, has_side_effects=True, vmem_limit_bytes=60 * 1024 * 1024
        ),
        cost_estimate=pl.CostEstimate(
            flops=flops, bytes_accessed=24 * 1024 * 1024, transcendentals=4 * 1024 * 1024
        ),
    )(
        trunk, norm_gain, head_bias, missing[None, :], group_ids.reshape(1, -1), group_weight,
        w_query, w_kv, w_out, w_up, skip, conv_w.reshape(taps * c2, c2), head_w, targets,
    )


def solution(mesh):
    in_specs = (
        P(("bin", "trk"), None), P(), P(), P(), P(), P(), P(("bin", "trk"), None), P(),
        P(None, "trk"), P("trk"), P("bin", "trk"), P("bin"), P(), P(),
    )
    out_specs = (P("bin", "trk"), P("bin", "trk"), P(("bin", "trk"), None))
    return jax.shard_map(body, mesh=mesh, in_specs=in_specs, out_specs=out_specs, check_vma=False)
```
